32 devices in a mesh: pole: 4 (over y, x), row: 2 (over core), col: 4 (over z).
Axes of the slice: x: 2, y: 2, z: 4, core: 2. Of those that a mesh axis runs over, the one named last changes fastest.
Arguments:
- hamiltonian_panel: bfloat16 [6144, 512], P(('row', 'col'), 'pole'), may hold values from -0.005859375 to 0.005859375
- margin_panel: bfloat16 [6144, 512], P(('row', 'col'), 'pole'), may hold values from -0.0029296875 to 0.0029296875
- shifts: float32 [4, 2], P('pole'), may hold values from -2 to 2
- weights: float32 [4, 2], P('pole'), may hold values from 0.5 to 2
- pivot_inverse: float32 [4, 2, 512, 512], P('pole'), may hold values from -6 to 6
- selected_inverse: bfloat16 [4, 2, 6144, 6144], P('pole', None, 'row', 'col'), may hold values from -6 to 6
Outputs:
- inverse_column: float32 [4, 6144, 2, 512], P('pole', ('row', 'col'))
- inverse_pivot: float32 [4, 2, 512, 512], P('pole')
- density_column: float32 [6144, 512], P(('row', 'col'), 'pole')
- density_pivot: float32 [512, 512], P('pole')
The draws below stay inside these ranges and needn't reach their ends.
All inputs are finite; a program needn't handle non-finite values.
Results may differ from the reference program's by a relative error of at most 0.0037.
Values may be sent and summed in bfloat16 or wider, within the bound.
A program may use at most 128 MiB of HBM per device.

```python
import math
import jax
import jax.numpy as jnp
from jax import lax

PANEL = 512
FRONT = 6144
POLES = 4


def with_spikes(values, rng, source, target, shards_of, factor):
    owner, partner = [(jnp.arange(values.shape[axis_at]) // (values.shape[axis_at] // shards_of)).reshape([-1 if axis == axis_at else 1 for axis in range(values.ndim)]) for axis_at in (source, target)]
    chosen = jax.random.permutation(rng, shards_of)[partner]
    strong = (owner == chosen) | (owner == (partner + shards_of // 2) % shards_of)
    return jnp.where(strong, factor * values, values)


def levels(own_key, shape, pieces, smallest, high):
    factor_of = 1.0
    for axis_at, shards_of in pieces:
        draws = jax.random.uniform(jax.random.fold_in(jax.random.fold_in(own_key, 6), axis_at), (shards_of,), jnp.float32, smallest / len(pieces), high / len(pieces))
        factor_of = factor_of * jnp.repeat(jnp.exp(draws), shape[axis_at] // shards_of).reshape((-1,) + (1,) * (len(shape) - 1 - axis_at))
    return factor_of


def scatter_about(own_key, extent, spread, most, shards=(), dtype=jnp.bfloat16):
    array = jax.random.normal(own_key, extent, jnp.float32) * spread
    if len(shards) > 0:
        array = levels(own_key, extent, shards, -0.22, 0.18) * array
    return jnp.clip(array, min=-most, max=most).astype(dtype)


def heavy_noise(key, shape, scale, bound, cuts, heavy, dtype=jnp.bfloat16):
    result = scale * jax.random.normal(key, shape, jnp.float32)
    if cuts:
        result = result * levels(key, shape, cuts, -0.22, 0.18)
    return jnp.clip(with_spikes(result, jax.random.fold_in(key, 3), *heavy), -bound, bound).astype(dtype)


def setup_inputs(seed: int = 0) -> dict:
    streams_of = jax.random.split(jax.random.key(seed), 7)
    hamiltonian_panel = scatter_about(streams_of[0], (FRONT, PANEL), ((2 * FRONT * PANEL) ** -0.5), 0.005859375, ((0, 8), (1, 4)))
    margin_panel = scatter_about(streams_of[1], (FRONT, PANEL), (0.5 * (2 * FRONT * PANEL) ** -0.5), 0.0029296875, ((0, 8), (1, 4)))
    shifts = jnp.clip(jax.random.uniform(streams_of[2], (POLES, 2), jnp.float32, -2.0, 2.0) * levels(streams_of[2], (POLES, 2), ((0, 4),), -0.4, 0.0), -2.0, 2.0)
    weights = jnp.clip(jnp.exp(math.log(2.0) - 1.3862944 * jax.random.uniform(streams_of[3], (POLES, 2), jnp.float32) ** levels(streams_of[3], (POLES, 2), ((0, 4),), -0.2, 0.2)), 0.5, 2.0)
    pivot_inverse = scatter_about(streams_of[4], (POLES, 2, PANEL, PANEL), 1.0, 6.0, ((0, 4),), jnp.float32)
    selected_inverse = heavy_noise(streams_of[5], (POLES, 2, FRONT, FRONT), 1.0, 6.0, ((0, 4), (2, 2), (3, 4)), (3, 2, 4, 2.0))
    return {"hamiltonian_panel": hamiltonian_panel, "margin_panel": margin_panel, "shifts": shifts, "weights": weights, "pivot_inverse": pivot_inverse, "selected_inverse": selected_inverse}


def precise(left, right):
    return jnp.dot(left, right, precision=lax.Precision.HIGHEST, preferred_element_type=jnp.float32)


def factor_panel(hamiltonian, margin, shift, inverse):
    hamiltonian_f = hamiltonian.astype(jnp.float32)
    margin_f = margin.astype(jnp.float32)
    real_part = hamiltonian_f - shift[0] * margin_f
    imag_part = -shift[1] * margin_f
    lower_real = precise(real_part, inverse[0]) - precise(imag_part, inverse[1])
    lower_imag = precise(real_part, inverse[1]) + precise(imag_part, inverse[0])
    return jnp.stack([lower_real, lower_imag], axis=1).astype(jnp.bfloat16)


def apply_block(block_real, block_imag, lower):
    width = lower.shape[2]
    flat = lower.reshape(lower.shape[0], 2 * width)
    first = jnp.dot(block_real, flat, preferred_element_type=jnp.float32)
    second = jnp.dot(block_imag, flat, preferred_element_type=jnp.float32)
    return -jnp.stack([first[:, :width] - second[:, width:], first[:, width:] + second[:, :width]], axis=1)


def pivot_term(lower, column):
    width = lower.shape[2]
    left = lower.astype(jnp.float32).reshape(lower.shape[0], 2 * width)
    right = column.reshape(column.shape[0], 2 * width)
    square = lax.dot_general(left, right, (((0,), (0,)), ((), ())), precision=lax.Precision.HIGHEST, preferred_element_type=jnp.float32)
    return jnp.stack([square[:width, :width] - square[width:, width:], square[:width, width:] + square[width:, :width]])


def reference(hamiltonian_panel, margin_panel, shifts, weights, pivot_inverse, selected_inverse):
    def one_pole(items):
        shift, weight, inverse, selected = items
        lower = factor_panel(hamiltonian_panel, margin_panel, shift, inverse)
        column = apply_block(selected[0], selected[1], lower)
        pivot = inverse - pivot_term(lower, column)
        column_density = weight[0] * column[:, 0] - weight[1] * column[:, 1]
        pivot_density = weight[0] * pivot[0] - weight[1] * pivot[1]
        return column, pivot, column_density, pivot_density

    columns, pivots, column_terms, pivot_terms = lax.map(one_pole, (shifts, weights, pivot_inverse, selected_inverse))
    return columns, pivots, jnp.sum(column_terms, axis=0), jnp.sum(pivot_terms, axis=0)
```

```python
import jax
import jax.numpy as jnp
from jax import lax
from jax.sharding import PartitionSpec as P

HALVES = 2


def precise(left, right):
    return jnp.dot(left, right, precision=lax.Precision.HIGH, preferred_element_type=jnp.float32)


def gather_panel(pair):
    return lax.all_gather(pair, "pole", axis=2, tiled=True)


def factor_panel(pair, shift, inverse):
    hamiltonian_f = pair[0].astype(jnp.float32)
    margin_f = pair[1].astype(jnp.float32)
    real_part = hamiltonian_f - shift[0] * margin_f
    imag_part = -shift[1] * margin_f
    lower_real = precise(real_part, inverse[0]) - precise(imag_part, inverse[1])
    lower_imag = precise(real_part, inverse[1]) + precise(imag_part, inverse[0])
    return lower_real.astype(jnp.bfloat16), lower_imag.astype(jnp.bfloat16)


def half_dot(left, right):
    return lax.dot_general(
        left, right, (((0,), (0,)), ((), ())), preferred_element_type=jnp.float32
    )


def body(hamiltonian_panel, margin_panel, shifts, weights, pivot_inverse, selected_inverse):
    shift = shifts[0]
    weight = weights[0]
    inverse = pivot_inverse[0]
    block_real = selected_inverse[0, 0]
    block_imag = selected_inverse[0, 1]
    n_row = lax.axis_size("row")
    n_col = lax.axis_size("col")
    n_pole = lax.axis_size("pole")
    width = inverse.shape[-1]
    part = width // HALVES

    own_pair = jnp.stack([hamiltonian_panel, margin_panel])
    order = [(n_row * c + r, r * n_col + c) for r in range(n_row) for c in range(n_col)]
    met_pair = gather_panel(lax.ppermute(own_pair, ("row", "col"), order))
    met_real, met_imag = factor_panel(met_pair, shift, inverse)

    partials = []
    for h in range(HALVES):
        cut = slice(h * part, (h + 1) * part)
        mine = jnp.concatenate([met_real[:, cut], met_imag[:, cut]], axis=1)
        rows = lax.all_gather(mine, "row", axis=0, tiled=True)
        turned = jnp.concatenate([rows[:, part:], -rows[:, :part]], axis=1)
        total = jnp.dot(block_imag, turned, preferred_element_type=jnp.float32) - jnp.dot(
            block_real, rows, preferred_element_type=jnp.float32
        )
        partials.append(total.astype(jnp.bfloat16))

    own_pair, partials[-1] = lax.optimization_barrier((own_pair, partials[-1]))
    own_real, own_imag = factor_panel(gather_panel(own_pair), shift, inverse)
    lower = jnp.concatenate([own_real, own_imag], axis=1)

    columns = []
    updates = []
    for h in range(HALVES):
        column = lax.psum_scatter(
            partials[h], "col", scatter_dimension=0, tiled=True
        ).astype(jnp.float32)
        high = column.astype(jnp.bfloat16)
        low = (column - high.astype(jnp.float32)).astype(jnp.bfloat16)
        square = half_dot(lower, high) + half_dot(lower, low)
        update = jnp.stack(
            [
                square[:width, :part] - square[width:, part:],
                square[:width, part:] + square[width:, :part],
            ]
        )
        updates.append(lax.psum(update, ("row", "col")))
        columns.append(column.reshape(column.shape[0], 2, part))
    column = jnp.concatenate(columns, axis=2)
    pivot = inverse - jnp.concatenate(updates, axis=2)

    column_density = weight[0] * column[:, 0] - weight[1] * column[:, 1]
    share = width // n_pole
    pieces = column_density.reshape(-1, n_pole, share).swapaxes(0, 1).astype(jnp.bfloat16)
    column_share = jnp.sum(
        lax.all_to_all(pieces, "pole", 0, 0, tiled=True).astype(jnp.float32), axis=0
    )
    pivot_density = weight[0] * pivot[0] - weight[1] * pivot[1]
    pieces = pivot_density.reshape(n_pole, share, width).astype(jnp.bfloat16)
    pivot_share = jnp.sum(
        lax.all_to_all(pieces, "pole", 0, 0, tiled=True).astype(jnp.float32), axis=0
    )
    return (column[None], pivot[None], column_share, pivot_share)


def solution(mesh):
    return jax.shard_map(
        body,
        mesh=mesh,
        in_specs=(
            P(("row", "col"), "pole"),
            P(("row", "col"), "pole"),
            P("pole", None),
            P("pole", None),
            P("pole", None, None, None),
            P("pole", None, "row", "col"),
        ),
        out_specs=(
            P("pole", ("row", "col"), None, None),
            P("pole", None, None, None),
            P(("row", "col"), "pole"),
            P("pole", None),
        ),
        check_vma=False,
    )
```

```python
import jax
import jax.numpy as jnp
from jax import lax
from jax.sharding import PartitionSpec as P

HALVES = 2


def precise(left, right):
    return jnp.dot(left, right, precision=lax.Precision.HIGH, preferred_element_type=jnp.float32)


def gather_panel(pair):
    rows = pair.shape[0] // 2
    return (
        lax.all_gather(pair[:rows], "pole", axis=1, tiled=True),
        lax.all_gather(pair[rows:], "pole", axis=1, tiled=True),
    )


def exchange_sum(pieces, axis):
    return jnp.sum(lax.all_to_all(pieces, axis, 0, 0, tiled=True).astype(jnp.float32), axis=0)


def factor_panel(pair, shift, inverse):
    hamiltonian_f = pair[0].astype(jnp.float32)
    margin_f = pair[1].astype(jnp.float32)
    real_part = hamiltonian_f - shift[0] * margin_f
    imag_part = -shift[1] * margin_f
    lower_real = precise(real_part, inverse[0]) - precise(imag_part, inverse[1])
    lower_imag = precise(real_part, inverse[1]) + precise(imag_part, inverse[0])
    return lower_real.astype(jnp.bfloat16), lower_imag.astype(jnp.bfloat16)


def half_dot(left, right):
    return lax.dot_general(
        left, right, (((0,), (0,)), ((), ())), preferred_element_type=jnp.float32
    )


def body(hamiltonian_panel, margin_panel, shifts, weights, pivot_inverse, selected_inverse):
    shift = shifts[0]
    weight = weights[0]
    inverse = pivot_inverse[0]
    block_real = selected_inverse[0, 0]
    block_imag = selected_inverse[0, 1]
    n_row = lax.axis_size("row")
    n_col = lax.axis_size("col")
    n_pole = lax.axis_size("pole")
    width = inverse.shape[-1]
    part = width // HALVES

    own_pair = jnp.concatenate([hamiltonian_panel, margin_panel], axis=0)
    order = [(n_row * c + r, r * n_col + c) for r in range(n_row) for c in range(n_col)]
    met_pair = gather_panel(lax.ppermute(own_pair, ("row", "col"), order))
    met_real, met_imag = factor_panel(met_pair, shift, inverse)

    partials = []
    for h in range(HALVES):
        cut = slice(h * part, (h + 1) * part)
        mine = jnp.concatenate([met_real[:, cut], met_imag[:, cut]], axis=1)
        rows = lax.all_gather(mine, "row", axis=0, tiled=True)
        turned = jnp.concatenate([rows[:, part:], -rows[:, :part]], axis=1)
        total = jnp.dot(block_imag, turned, preferred_element_type=jnp.float32) - jnp.dot(
            block_real, rows, preferred_element_type=jnp.float32
        )
        partials.append(total.astype(jnp.bfloat16))

    own_pair, partials[-1] = lax.optimization_barrier((own_pair, partials[-1]))
    own_real, own_imag = factor_panel(gather_panel(own_pair), shift, inverse)
    lower = jnp.concatenate([own_real, own_imag], axis=1)

    columns = []
    updates = []
    for h in range(HALVES):
        column = exchange_sum(partials[h].reshape(n_col, -1, 2 * part), "col")
        high = column.astype(jnp.bfloat16)
        low = (column - high.astype(jnp.float32)).astype(jnp.bfloat16)
        square = half_dot(lower, high) + half_dot(lower, low)
        update = jnp.stack(
            [
                square[:width, :part] - square[width:, part:],
                square[:width, part:] + square[width:, :part],
            ]
        )
        updates.append(update)
        columns.append(column.reshape(column.shape[0], 2, part))
    column = jnp.concatenate(columns, axis=2)
    update = jnp.concatenate(updates, axis=2)
    pieces = update.reshape(n_row * n_col, -1, width).astype(jnp.bfloat16)
    piece = lax.optimization_barrier(exchange_sum(pieces, ("row", "col")))
    update = lax.all_gather(piece.astype(jnp.bfloat16), ("row", "col"), axis=0, tiled=True)
    pivot = inverse - update.reshape(2, width, width).astype(jnp.float32)

    column_density = weight[0] * column[:, 0] - weight[1] * column[:, 1]
    share = width // n_pole
    column_share = exchange_sum(
        column_density.reshape(-1, n_pole, share).swapaxes(0, 1), "pole"
    )
    pivot_density = weight[0] * pivot[0] - weight[1] * pivot[1]
    pivot_share = exchange_sum(pivot_density.reshape(n_pole, share, width), "pole")
    return (column[None], pivot[None], column_share, pivot_share)


def solution(mesh):
    return jax.shard_map(
        body,
        mesh=mesh,
        in_specs=(
            P(("row", "col"), "pole"),
            P(("row", "col"), "pole"),
            P("pole", None),
            P("pole", None),
            P("pole", None, None, None),
            P("pole", None, "row", "col"),
        ),
        out_specs=(
            P("pole", ("row", "col"), None, None),
            P("pole", None, None, None),
            P(("row", "col"), "pole"),
            P("pole", None),
        ),
        check_vma=False,
    )
```

```python
import jax
import jax.numpy as jnp
from jax import lax
from jax.sharding import PartitionSpec as P

HALVES = 2


def precise(left, right):
    return jnp.dot(left, right, precision=lax.Precision.HIGH, preferred_element_type=jnp.float32)


def gather_panel(pair):
    rows = pair.shape[0] // 2
    return (
        lax.all_gather(pair[:rows], "pole", axis=1, tiled=True),
        lax.all_gather(pair[rows:], "pole", axis=1, tiled=True),
    )


def exchange_sum(pieces, axis):
    return jnp.sum(lax.all_to_all(pieces, axis, 0, 0, tiled=True).astype(jnp.float32), axis=0)


def factor_panel(pair, shift, inverse):
    hamiltonian_f = pair[0].astype(jnp.float32)
    margin_f = pair[1].astype(jnp.float32)
    real_part = hamiltonian_f - shift[0] * margin_f
    imag_part = -shift[1] * margin_f
    lower_real = precise(real_part, inverse[0]) - precise(imag_part, inverse[1])
    lower_imag = precise(real_part, inverse[1]) + precise(imag_part, inverse[0])
    return lower_real.astype(jnp.bfloat16), lower_imag.astype(jnp.bfloat16)


def half_dot(left, right):
    return lax.dot_general(
        left, right, (((0,), (0,)), ((), ())), preferred_element_type=jnp.float32
    )


def body(hamiltonian_panel, margin_panel, shifts, weights, pivot_inverse, selected_inverse):
    shift = shifts[0]
    weight = weights[0]
    inverse = pivot_inverse[0]
    block_real = selected_inverse[0, 0]
    block_imag = selected_inverse[0, 1]
    n_row = lax.axis_size("row")
    n_col = lax.axis_size("col")
    n_pole = lax.axis_size("pole")
    width = inverse.shape[-1]
    part = width // HALVES

    own_pair = jnp.concatenate([hamiltonian_panel, margin_panel], axis=0)
    order = [(n_row * c + r, r * n_col + c) for r in range(n_row) for c in range(n_col)]
    met_pair = gather_panel(lax.ppermute(own_pair, ("row", "col"), order))
    met_real, met_imag = factor_panel(met_pair, shift, inverse)

    cuts = [slice(h * part, (h + 1) * part) for h in range(HALVES)]
    mine = jnp.concatenate([side[:, cut] for cut in cuts for side in (met_real, met_imag)], axis=1)
    met = lax.all_gather(mine, "row", axis=0, tiled=True)

    partials = []
    for h in range(HALVES):
        rows = met[:, 2 * h * part : 2 * (h + 1) * part]
        turned = jnp.concatenate([rows[:, part:], -rows[:, :part]], axis=1)
        total = jnp.dot(block_imag, turned, preferred_element_type=jnp.float32) - jnp.dot(
            block_real, rows, preferred_element_type=jnp.float32
        )
        partials.append(total.astype(jnp.bfloat16))

    own_pair, partials[-1] = lax.optimization_barrier((own_pair, partials[-1]))
    own_real, own_imag = factor_panel(gather_panel(own_pair), shift, inverse)
    lower = jnp.concatenate([own_real, own_imag], axis=1)

    columns = []
    updates = []
    for h in range(HALVES):
        column = exchange_sum(partials[h].reshape(n_col, -1, 2 * part), "col")
        high = column.astype(jnp.bfloat16)
        low = (column - high.astype(jnp.float32)).astype(jnp.bfloat16)
        square = half_dot(lower, high) + half_dot(lower, low)
        update = jnp.stack(
            [
                square[:width, :part] - square[width:, part:],
                square[:width, part:] + square[width:, :part],
            ]
        )
        updates.append(update)
        columns.append(column.reshape(column.shape[0], 2, part))
    column = jnp.concatenate(columns, axis=2)
    update = jnp.concatenate(updates, axis=2)
    pieces = update.reshape(n_row * n_col, -1, width).astype(jnp.bfloat16)
    piece = lax.optimization_barrier(exchange_sum(pieces, ("row", "col")))
    update = lax.all_gather(piece.astype(jnp.bfloat16), ("row", "col"), axis=0, tiled=True)
    pivot = inverse - update.reshape(2, width, width).astype(jnp.float32)

    column_density = weight[0] * column[:, 0] - weight[1] * column[:, 1]
    share = width // n_pole
    column_share = exchange_sum(
        column_density.reshape(-1, n_pole, share).swapaxes(0, 1), "pole"
    )
    pivot_density = weight[0] * pivot[0] - weight[1] * pivot[1]
    pivot_share = exchange_sum(pivot_density.reshape(n_pole, share, width), "pole")
    return (column[None], pivot[None], column_share, pivot_share)


def solution(mesh):
    return jax.shard_map(
        body,
        mesh=mesh,
        in_specs=(
            P(("row", "col"), "pole"),
            P(("row", "col"), "pole"),
            P("pole", None),
            P("pole", None),
            P("pole", None, None, None),
            P("pole", None, "row", "col"),
        ),
        out_specs=(
            P("pole", ("row", "col"), None, None),
            P("pole", None, None, None),
            P(("row", "col"), "pole"),
            P("pole", None),
        ),
        check_vma=False,
    )
```

```python
import jax
import jax.numpy as jnp
from jax import lax
from jax.sharding import PartitionSpec as P

HALVES = 2


def precise(left, right):
    return jnp.dot(left, right, precision=lax.Precision.HIGH, preferred_element_type=jnp.float32)


def gather_panel(pair):
    rows = pair.shape[0] // 2
    return (
        lax.all_gather(pair[:rows], "pole", axis=1, tiled=True),
        lax.all_gather(pair[rows:], "pole", axis=1, tiled=True),
    )


def exchange_sum(pieces, axis):
    return jnp.sum(lax.all_to_all(pieces, axis, 0, 0, tiled=True).astype(jnp.float32), axis=0)


def factor_panel(pair, shift, inverse):
    hamiltonian_f = pair[0].astype(jnp.float32)
    margin_f = pair[1].astype(jnp.float32)
    real_part = hamiltonian_f - shift[0] * margin_f
    imag_part = -shift[1] * margin_f
    lower_real = precise(real_part, inverse[0]) - precise(imag_part, inverse[1])
    lower_imag = precise(real_part, inverse[1]) + precise(imag_part, inverse[0])
    return lower_real.astype(jnp.bfloat16), lower_imag.astype(jnp.bfloat16)


def half_dot(left, right):
    return lax.dot_general(
        left, right, (((0,), (0,)), ((), ())), preferred_element_type=jnp.float32
    )


def body(hamiltonian_panel, margin_panel, shifts, weights, pivot_inverse, selected_inverse):
    shift = shifts[0]
    weight = weights[0]
    inverse = pivot_inverse[0]
    block_real = selected_inverse[0, 0]
    block_imag = selected_inverse[0, 1]
    n_row = lax.axis_size("row")
    n_col = lax.axis_size("col")
    n_pole = lax.axis_size("pole")
    width = inverse.shape[-1]
    part = width // HALVES

    own_pair = jnp.concatenate([hamiltonian_panel, margin_panel], axis=0)
    order = [(n_row * c + r, r * n_col + c) for r in range(n_row) for c in range(n_col)]
    met_pair = gather_panel(lax.ppermute(own_pair, ("row", "col"), order))
    met_real, met_imag = factor_panel(met_pair, shift, inverse)

    partials = []
    for h in range(HALVES):
        cut = slice(h * part, (h + 1) * part)
        mine = jnp.concatenate([met_real[:, cut], met_imag[:, cut]], axis=1)
        copies = jnp.broadcast_to(mine[None], (n_row,) + mine.shape)
        rows = lax.all_to_all(copies, "row", 0, 0, tiled=True).reshape(-1, 2 * part)
        turned = jnp.concatenate([rows[:, part:], -rows[:, :part]], axis=1)
        total = jnp.dot(block_imag, turned, preferred_element_type=jnp.float32) - jnp.dot(
            block_real, rows, preferred_element_type=jnp.float32
        )
        partials.append(total.astype(jnp.bfloat16))

    own_pair, partials[-1] = lax.optimization_barrier((own_pair, partials[-1]))
    own_real, own_imag = factor_panel(gather_panel(own_pair), shift, inverse)
    lower = jnp.concatenate([own_real, own_imag], axis=1)

    columns = []
    updates = []
    for h in range(HALVES):
        column = exchange_sum(partials[h].reshape(n_col, -1, 2 * part), "col")
        high = column.astype(jnp.bfloat16)
        low = (column - high.astype(jnp.float32)).astype(jnp.bfloat16)
        square = half_dot(lower, high) + half_dot(lower, low)
        update = jnp.stack(
            [
                square[:width, :part] - square[width:, part:],
                square[:width, part:] + square[width:, :part],
            ]
        )
        updates.append(update)
        columns.append(column.reshape(column.shape[0], 2, part))
    column = jnp.concatenate(columns, axis=2)
    update = jnp.concatenate(updates, axis=2)
    near = exchange_sum(update.reshape(n_row, -1, width), "row")
    far = near.reshape(n_col, -1, width).astype(jnp.bfloat16)
    piece = lax.optimization_barrier(exchange_sum(far, "col"))
    update = lax.all_gather(piece.astype(jnp.bfloat16), ("row", "col"), axis=0, tiled=True)
    pivot = inverse - update.reshape(2, width, width).astype(jnp.float32)

    column_density = weight[0] * column[:, 0] - weight[1] * column[:, 1]
    share = width // n_pole
    column_share = exchange_sum(
        column_density.reshape(-1, n_pole, share).swapaxes(0, 1), "pole"
    )
    pivot_density = weight[0] * pivot[0] - weight[1] * pivot[1]
    pivot_share = exchange_sum(pivot_density.reshape(n_pole, share, width), "pole")
    return (column[None], pivot[None], column_share, pivot_share)


def solution(mesh):
    return jax.shard_map(
        body,
        mesh=mesh,
        in_specs=(
            P(("row", "col"), "pole"),
            P(("row", "col"), "pole"),
            P("pole", None),
            P("pole", None),
            P("pole", None, None, None),
            P("pole", None, "row", "col"),
        ),
        out_specs=(
            P("pole", ("row", "col"), None, None),
            P("pole", None, None, None),
            P(("row", "col"), "pole"),
            P("pole", None),
        ),
        check_vma=False,
    )
```
